32 devices in a mesh: blk: 4 (over y, core), reader: 2 (over x), bulk: 4 (over z).
Axes of the slice: x: 2, y: 2, z: 4, core: 2. Of those that a mesh axis runs over, the one named last changes fastest.
Arguments:
- vectors: float32 [128, 8192], P('bulk', ('blk', 'reader')), may hold values from -6 to 6
- ham_tiles: float32 [8, 4, 24, 128, 128], P(('blk', 'reader'))
- tile_rows: int32 [8, 4, 24], P(('blk', 'reader')), may hold values from 0 to 7, as said below
- tile_cols: int32 [8, 4, 24], P(('blk', 'reader')), may hold values from 0 to 15
- center: float32 [1], replicated, may hold values from -0.5 to 0.5
- halfwidth: float32 [1], replicated, may hold values from 1 to 2
Outputs:
- filtered: float32 [128, 8192], P('bulk', ('blk', 'reader'))
The draws below stay inside these ranges and needn't reach their ends.
Inputs may be any that keep to these rules, and one draw needn't show every extreme that they name: tile_rows and tile_cols of one panel together name 24 different tiles.
All inputs are finite; a program needn't handle non-finite values.
Results may differ from the reference program's by a relative error of at most 0.0003.
Values sent between devices are 32-bit elements; how exact they have to be, the bound alone decides.
A program may use at most 64 MiB of HBM per device.

```python
import jax
import jax.numpy as jnp
from jax import lax

VECS = 128
TILE = 128
RT = 8
PT = 24
PASSES = 2
NBLOCKS = 8
NROWS = 8192
N_BLK = 4
N_READER = 2


def pattern_draw(key):
    inner = jax.random.fold_in(key, 7)
    total = N_READER * RT * RT
    panels = NBLOCKS * N_BLK
    keys = jax.random.split(inner, panels)
    perms = jax.vmap(lambda k: jax.random.permutation(k, total))(keys)[:, :PT].astype(jnp.int32)
    panel_ids = jnp.arange(panels, dtype=jnp.int32)
    moved = jnp.where(panel_ids % 2 == 0, total - 1 - perms[:, 0], total - perms[:, 0])
    places = (perms + moved[:, None]) % total
    places = places.reshape(NBLOCKS, N_BLK, PT)
    return (places // (N_READER * RT), places % (N_READER * RT))


def draw_tile_rows(key, part):
    return pattern_draw(key)[0].astype(jnp.int32)


def draw_tile_cols(key, part):
    return pattern_draw(key)[1].astype(jnp.int32)


def draw_ham_tiles(key, part):
    shape = (NBLOCKS, N_BLK, PT, TILE, TILE)
    first = jax.random.fold_in(jax.random.fold_in(key, 11), 0)
    fan = TILE * N_BLK * PT / RT
    rising = 3.0 ** (jnp.arange(NBLOCKS, dtype=jnp.float32) / (NBLOCKS - 1))
    rising = rising.reshape(NBLOCKS, 1, 1, 1, 1)
    base = jax.random.normal(first, shape, jnp.float32)
    return (base * rising / jnp.sqrt(fan)).astype(jnp.float32)


def levels(own_key, dims, shards, least, top_value):
    gain = 1.0
    for dim, shards_of in shards:
        draws = jax.random.uniform(jax.random.fold_in(jax.random.fold_in(own_key, 6), dim), (shards_of,), jnp.float32, least / len(shards), top_value / len(shards))
        gain = gain * jnp.repeat(jnp.exp(draws), dims[dim] // shards_of).reshape((-1,) + (1,) * (len(dims) - 1 - dim))
    return gain


def bell_draw(own_key, extent, scale, bound, shards=(), kind=jnp.bfloat16):
    loudness = levels(own_key, extent, shards, -0.22, 0.18) if shards else 1.0
    array = jax.random.normal(own_key, extent, jnp.float32) * scale * loudness
    return jnp.minimum(jnp.maximum(array, -bound), bound).astype(kind)


def setup_inputs(seed: int = 0) -> dict:
    key_of = jax.random.split(jax.random.key(seed), 7)
    return {
        "vectors": bell_draw(key_of[0], (VECS, NROWS), 1.0, 6.0, ((0, 4), (1, 8)), jnp.float32),
        "ham_tiles": draw_ham_tiles(jax.random.fold_in(key_of[6], 71), 0),
        "tile_rows": draw_tile_rows(jax.random.fold_in(key_of[6], 71), 0),
        "tile_cols": draw_tile_cols(jax.random.fold_in(key_of[6], 71), 0),
        "center": jnp.clip(jax.random.uniform(key_of[4], (1,), jnp.float32, -0.5, 0.5), -0.5, 0.5),
        "halfwidth": jnp.clip(jax.random.uniform(key_of[5], (1,), jnp.float32, 1.0, 2.0), 1.0, 2.0),
    }


def contribute(sources, tiles, rows, count):
    prod = jnp.einsum('vkc,krc->vkr', sources, tiles, precision=lax.Precision.HIGHEST)
    onehot = (rows[:, None] == jnp.arange(count, dtype=jnp.int32)[None, :]).astype(jnp.float32)
    return jnp.einsum('vkr,kt->vtr', prod, onehot, precision=lax.Precision.HIGHEST)

def apply_ham(current, ham_tiles, tile_rows, tile_cols):
    tiled = current.reshape(VECS, NBLOCKS * RT, TILE)
    offsets = (jnp.arange(N_BLK, dtype=jnp.int32) * (N_READER * RT))[:, None]

    def one_block(items):
        tiles, rows, cols = items
        glob = (offsets + cols).reshape(-1).astype(jnp.int32)
        sources = jnp.take(tiled, glob, axis=1)
        return contribute(sources, tiles.reshape(N_BLK * PT, TILE, TILE), rows.reshape(-1), RT)
    blocks = lax.map(one_block, (ham_tiles, tile_rows, tile_cols))
    return jnp.transpose(blocks, (1, 0, 2, 3)).reshape(VECS, NBLOCKS * RT * TILE)

def reference(vectors, ham_tiles, tile_rows, tile_cols, center, halfwidth):

    def scaled(v):
        return (apply_ham(v, ham_tiles, tile_rows, tile_cols) - center[0] * v) / halfwidth[0]
    current = vectors
    for step in range(PASSES):
        first = scaled(current)
        second = 2.0 * scaled(first) - current
        third = 2.0 * scaled(second) - first
        sq = lax.optimization_barrier(jnp.sum(third * third, axis=1))
        current = third / jnp.sqrt(sq / NROWS + 1e-06)[:, None]
    return current
```

```python
import functools

import jax
import jax.numpy as jnp
from jax import lax
from jax.experimental import pallas as pl
from jax.experimental.pallas import tpu as pltpu
from jax.sharding import PartitionSpec as P

TILE = 128
PASSES = 2
DEGREE = 3
CORES = 2


def kernel(
    n_blk, n_reader, total_cols,
    vec_ref, ham_ref, rows_ref, cols_ref, center_ref, half_ref,
    out_ref,
    blocks, sources, staged, weights, acc, before, scale, sums, partial_sum,
    ham_sem,
    send_x, send_y, send_dx, send_dy, send_own, send_cx, send_cy, send_cdx, send_cdy,
    recv_x, recv_y, recv_dx, recv_dy, recv_own, recv_cx, recv_cy, recv_cdx, recv_cdy,
    send_sum, recv_sum,
):
    vecs = vec_ref.shape[0]
    row_tiles = vec_ref.shape[1] // TILE
    slots = rows_ref.shape[2]
    group_tiles = n_reader * row_tiles
    peers = n_blk * n_reader - 1
    half = vecs // 2
    halves = (pl.ds(0, half), pl.ds(half, half))

    blk = lax.axis_index("blk")
    x = lax.axis_index("reader")
    core = lax.rem(blk, CORES)
    side = blk - core
    blk_c = side + (1 - core)
    blk_y = lax.rem(blk + CORES, n_blk)
    blk_yc = lax.rem(blk_c + CORES, n_blk)
    me = blk * n_reader + x

    def peer(step):
        other = lax.rem(me + step, n_blk * n_reader)
        return {"blk": other // n_reader, "reader": lax.rem(other, n_reader)}

    def block_of(b, step=0):
        return b * n_reader + lax.rem(x + n_reader - step, n_reader)

    barrier = pltpu.get_barrier_semaphore()
    for step in range(1, peers + 1):
        pl.semaphore_signal(
            barrier, inc=1, device_id=peer(step), device_id_type=pl.DeviceIdType.MESH
        )

    def ham_copy(group):
        return pltpu.make_async_copy(
            ham_ref.at[0, group], staged.at[group], ham_sem.at[group]
        )

    for group in (blk, blk_c, blk_y, blk_yc):
        ham_copy(group).start()
    blocks[0, me] = vec_ref[...]
    scale[...] = jnp.ones_like(scale)
    before[...] = jnp.zeros_like(before)
    pl.semaphore_wait(barrier, peers)

    def split_tiles(group):
        ham_copy(group).wait()

        def one(slot, carry):
            tile = staged[group, slot]
            high = tile.astype(jnp.bfloat16)
            low = (tile - high.astype(jnp.float32)).astype(jnp.bfloat16)
            weights[group * slots + slot] = jnp.concatenate([high, low], axis=1)
            return carry

        lax.fori_loop(0, slots, one, 0)

    def split_block(par, index):
        for t in range(row_tiles):
            value = blocks[par, index, :, t * TILE : (t + 1) * TILE] * scale[...]
            high = value.astype(jnp.bfloat16)
            low = (value - high.astype(jnp.float32)).astype(jnp.bfloat16)
            sources[index * row_tiles + t] = jnp.concatenate([high, low], axis=0)

    unroll = max(u for u in (8, 6, 4, 3, 2, 1) if slots % u == 0)

    def multiply(group):
        def some(turn, carry):
            carry = list(carry)
            for u in range(unroll):
                slot = turn * unroll + u
                col = cols_ref[0, group, slot]
                row = rows_ref[0, group, slot]
                source = sources[group * group_tiles + col]
                product = lax.dot_general(
                    jnp.concatenate([source, source], axis=1),
                    weights[group * slots + slot],
                    (((1,), (1,)), ((), ())),
                    preferred_element_type=jnp.float32,
                )
                product = product[:vecs] + product[vecs:]
                for t in range(row_tiles):
                    carry[t] = carry[t] + jnp.where(row == t, product, 0.0)
            return tuple(carry)

        start = tuple(acc[t] for t in range(row_tiles))
        done = lax.fori_loop(0, slots // unroll, some, start)
        for t in range(row_tiles):
            acc[t] = done[t]

    def remote(par, index, part, send, recv, target):
        where = blocks.at[par, index] if part is None else blocks.at[par, index, halves[part]]
        return pltpu.make_async_remote_copy(
            src_ref=where, dst_ref=where, send_sem=send, recv_sem=recv,
            device_id=target, device_id_type=pl.DeviceIdType.MESH,
        )

    to_core = {"blk": blk_c}
    to_y = {"blk": blk_y}

    def to_x(step):
        return {"reader": lax.rem(x + step, n_reader)}

    steps = range(1, n_reader)

    def sum_copy(turn, step):
        return pltpu.make_async_remote_copy(
            src_ref=partial_sum.at[turn], dst_ref=sums.at[turn, step - 1],
            send_sem=send_sum.at[turn, step - 1], recv_sem=recv_sum.at[turn, step - 1],
            device_id=peer(step), device_id_type=pl.DeviceIdType.MESH,
        )

    diagonal = (
        lax.broadcasted_iota(jnp.int32, (vecs, TILE), 0)
        == lax.broadcasted_iota(jnp.int32, (vecs, TILE), 1)
    )

    def share_sums(turn, squares):
        own = jnp.sum(squares, axis=1, keepdims=True)
        line = jnp.sum(jnp.where(diagonal, own, 0.0), axis=0, keepdims=True)
        partial_sum[turn] = jnp.broadcast_to(line, partial_sum.shape[1:])
        for step in range(1, peers + 1):
            sum_copy(turn, step).start()

    def norms(turn):
        for step in range(1, peers + 1):
            sum_copy(turn, step).wait()
        total = partial_sum[turn]
        for step in range(1, peers + 1):
            total = total + sums[turn, step - 1]
        spread = jnp.broadcast_to(total[:1], (vecs, TILE))
        squares = jnp.sum(jnp.where(diagonal, spread, 0.0), axis=1, keepdims=True)
        root = jnp.sqrt(squares / total_cols + 1e-06)
        return jnp.broadcast_to(1.0 / root, (vecs, TILE))

    def apply(k, carry):
        par = lax.rem(k, 2)
        x_own = [[remote(par, me, h, send_x.at[s - 1, h], recv_x.at[par, s - 1, h], to_x(s))
                  for h in range(2)] for s in steps]
        y_own = [remote(par, me, h, send_y.at[h], recv_y.at[par, h], to_y) for h in range(2)]
        c_own = remote(par, me, None, send_own, recv_own.at[par], to_core)
        x_block = [block_of(blk, s) for s in steps]
        y_block = block_of(blk_y)
        d_block = [block_of(blk_y, s) for s in steps]
        dy = [remote(par, x_block[s - 1], 0, send_dy.at[s - 1], recv_dy.at[par, s - 1], to_y)
              for s in steps]
        dx = [remote(par, y_block, 1, send_dx.at[s - 1], recv_dx.at[par, s - 1], to_x(s))
              for s in steps]
        cx = [[remote(par, x_block[s - 1], h, send_cx.at[s - 1, h],
                      recv_cx.at[par, s - 1, h], to_core) for h in range(2)] for s in steps]
        cy = [remote(par, y_block, h, send_cy.at[h], recv_cy.at[par, h], to_core)
              for h in range(2)]
        cdy = [remote(par, d_block[s - 1], 0, send_cdy.at[s - 1], recv_cdy.at[par, s - 1],
                      to_core) for s in steps]
        cdx = [remote(par, d_block[s - 1], 1, send_cdx.at[s - 1], recv_cdx.at[par, s - 1],
                      to_core) for s in steps]

        for s in steps:
            x_own[s - 1][0].start()
        y_own[1].start()
        c_own.start()
        for s in steps:
            x_own[s - 1][1].start()
        y_own[0].start()

        acc[...] = jnp.zeros_like(acc)

        @pl.when(k == 0)
        def _():
            split_tiles(blk)
            split_tiles(blk_c)

        @pl.when(k == DEGREE)
        def _():
            scale[...] = norms(0)

        @pl.when(k == DEGREE + 1)
        def _():
            scale[...] = jnp.ones_like(scale)

        split_block(par, me)
        for s in steps:
            x_own[s - 1][0].wait_recv()
            dy[s - 1].start()
            cx[s - 1][0].start()
        y_own[1].wait_recv()
        for s in steps:
            dx[s - 1].start()
        cy[1].start()
        for s in steps:
            x_own[s - 1][1].wait_recv()
            cx[s - 1][1].start()
            split_block(par, x_block[s - 1])
        y_own[0].wait_recv()
        cy[0].start()
        split_block(par, y_block)
        c_own.wait_recv()
        split_block(par, block_of(blk_c))
        multiply(blk)

        @pl.when(k == 0)
        def _():
            split_tiles(blk_y)
            split_tiles(blk_yc)

        for s in steps:
            dy[s - 1].wait_recv()
            cdy[s - 1].start()
            dx[s - 1].wait_recv()
            cdx[s - 1].start()
            split_block(par, d_block[s - 1])
        for s in steps:
            cx[s - 1][0].wait_recv()
            cx[s - 1][1].wait_recv()
            split_block(par, block_of(blk_c, s))
        multiply(blk_c)
        multiply(blk_y)
        cy[1].wait_recv()
        cy[0].wait_recv()
        split_block(par, block_of(blk_yc))
        for s in steps:
            cdy[s - 1].wait_recv()
            cdx[s - 1].wait_recv()
            split_block(par, block_of(blk_yc, s))
        multiply(blk_yc)

        first = lax.rem(k, DEGREE) == 0
        center = center_ref[0]
        gain = jnp.where(first, 1.0, 2.0) / half_ref[0]
        squares = jnp.zeros((vecs, TILE), jnp.float32)
        for t in range(row_tiles):
            lanes = slice(t * TILE, (t + 1) * TILE)
            field = blocks[par, me, :, lanes] * scale[...]
            new = (acc[t] - center * field) * gain
            new = new - jnp.where(first, 0.0, before[:, lanes])
            before[:, lanes] = field
            blocks[1 - par, me, :, lanes] = new
            squares = squares + new * new

        @pl.when(lax.rem(k, DEGREE) == DEGREE - 1)
        def _():
            share_sums(k // DEGREE, squares)

        c_own.wait_send()
        for h in range(2):
            y_own[h].wait_send()
            cy[h].wait_send()
        for s in steps:
            for h in range(2):
                x_own[s - 1][h].wait_send()
                cx[s - 1][h].wait_send()
            for copy in (dx, dy, cdx, cdy):
                copy[s - 1].wait_send()
        return carry

    lax.fori_loop(0, PASSES * DEGREE, apply, 0)
    last = norms(PASSES - 1)
    for t in range(row_tiles):
        lanes = slice(t * TILE, (t + 1) * TILE)
        out_ref[:, lanes] = blocks[PASSES * DEGREE % 2, me, :, lanes] * last


def shards(n_blk, n_reader, vectors, ham_tiles, tile_rows, tile_cols, center, halfwidth):
    vecs, width = vectors.shape
    row_tiles = width // TILE
    n = n_blk * n_reader
    groups, slots = tile_rows.shape[1:]
    others = n_reader - 1
    dma = pltpu.SemaphoreType.DMA
    smem = pl.BlockSpec(memory_space=pltpu.SMEM)
    vmem = pl.BlockSpec(memory_space=pltpu.VMEM)
    body = functools.partial(kernel, n_blk, n_reader, n * width)
    return pl.pallas_call(
        body,
        out_shape=jax.ShapeDtypeStruct((vecs, width), jnp.float32),
        in_specs=[vmem, pl.BlockSpec(memory_space=pl.ANY), smem, smem, smem, smem],
        out_specs=vmem,
        scratch_shapes=[
            pltpu.VMEM((2, n, vecs, width), jnp.float32),
            pltpu.VMEM((n * row_tiles, 2 * vecs, TILE), jnp.bfloat16),
            pltpu.VMEM((groups, slots, TILE, TILE), jnp.float32),
            pltpu.VMEM((groups * slots, TILE, 2 * TILE), jnp.bfloat16),
            pltpu.VMEM((row_tiles, vecs, TILE), jnp.float32),
            pltpu.VMEM((vecs, width), jnp.float32),
            pltpu.VMEM((vecs, TILE), jnp.float32),
            pltpu.VMEM((PASSES, n - 1, 8, TILE), jnp.float32),
            pltpu.VMEM((PASSES, 8, TILE), jnp.float32),
            dma((groups,)),
            dma((others, 2)), dma((2,)), dma((others,)), dma((others,)), dma,
            dma((others, 2)), dma((2,)), dma((others,)), dma((others,)),
            dma((2, others, 2)), dma((2, 2)), dma((2, others)), dma((2, others)), dma((2,)),
            dma((2, others, 2)), dma((2, 2)), dma((2, others)), dma((2, others)),
            dma((PASSES, n - 1)), dma((PASSES, n - 1)),
        ],
        compiler_params=pltpu.CompilerParams(
            collective_id=0, has_side_effects=True, vmem_limit_bytes=48 * 2**20
        ),
        cost_estimate=pl.CostEstimate(
            flops=PASSES * DEGREE * groups * slots * 8 * vecs * TILE * TILE,
            bytes_accessed=groups * slots * TILE * TILE * 4,
            transcendentals=0,
        ),
    )(vectors, ham_tiles, tile_rows, tile_cols, center, halfwidth)


def solution(mesh):
    n_blk, n_reader = mesh.shape["blk"], mesh.shape["reader"]
    return jax.shard_map(
        functools.partial(shards, n_blk, n_reader),
        mesh=mesh,
        in_specs=(
            P("bulk", ("blk", "reader")),
            P(("blk", "reader"), None, None, None, None),
            P(("blk", "reader"), None, None),
            P(("blk", "reader"), None, None),
            P(),
            P(),
        ),
        out_specs=P("bulk", ("blk", "reader")),
        check_vma=False,
    )
```

```python
import functools

import jax
import jax.numpy as jnp
from jax import lax
from jax.experimental import pallas as pl
from jax.experimental.pallas import tpu as pltpu
from jax.sharding import PartitionSpec as P

TILE = 128
PASSES = 2
DEGREE = 3
CORES = 2


def kernel(
    n_blk, n_reader, total_cols,
    vec_ref, ham_ref, rows_ref, cols_ref, center_ref, half_ref,
    out_ref,
    blocks, sources, staged, weights, acc, before, scale, sums, partial_sum,
    rows_smem, cols_smem, ham_sem, in_sem,
    send_x, send_y, send_dx, send_dy, send_own, send_cx, send_cy, send_cdx, send_cdy,
    recv_x, recv_y, recv_dx, recv_dy, recv_own, recv_cx, recv_cy, recv_cdx, recv_cdy,
    send_sum, recv_sum,
):
    vecs = vec_ref.shape[0]
    row_tiles = vec_ref.shape[1] // TILE
    slots = rows_ref.shape[2]
    group_tiles = n_reader * row_tiles
    peers = n_blk * n_reader - 1
    half = vecs // 2
    halves = (pl.ds(0, half), pl.ds(half, half))

    blk = lax.axis_index("blk")
    x = lax.axis_index("reader")
    core = lax.rem(blk, CORES)
    side = blk - core
    blk_c = side + (1 - core)
    blk_y = lax.rem(blk + CORES, n_blk)
    blk_yc = lax.rem(blk_c + CORES, n_blk)
    me = blk * n_reader + x

    def peer(step):
        other = lax.rem(me + step, n_blk * n_reader)
        return {"blk": other // n_reader, "reader": lax.rem(other, n_reader)}

    def block_of(b, step=0):
        return b * n_reader + lax.rem(x + n_reader - step, n_reader)

    barrier = pltpu.get_barrier_semaphore()
    for step in range(1, peers + 1):
        pl.semaphore_signal(
            barrier, inc=1, device_id=peer(step), device_id_type=pl.DeviceIdType.MESH
        )

    def ham_copy(group):
        return pltpu.make_async_copy(
            ham_ref.at[0, group], staged.at[group], ham_sem.at[group]
        )

    loads = [
        pltpu.make_async_copy(vec_ref, blocks.at[0, me], in_sem.at[0]),
        pltpu.make_async_copy(rows_ref.at[0], rows_smem, in_sem.at[1]),
        pltpu.make_async_copy(cols_ref.at[0], cols_smem, in_sem.at[2]),
    ]
    for copy in loads:
        copy.start()
    for group in (blk, blk_c, blk_y, blk_yc):
        ham_copy(group).start()
    scale[...] = jnp.ones_like(scale)
    before[...] = jnp.zeros_like(before)
    for copy in loads:
        copy.wait()
    pl.semaphore_wait(barrier, peers)

    def split_tiles(group):
        ham_copy(group).wait()

        def one(slot, carry):
            tile = staged[group, slot].T
            high = tile.astype(jnp.bfloat16)
            low = (tile - high.astype(jnp.float32)).astype(jnp.bfloat16)
            weights[group * slots + slot] = jnp.concatenate([high, low], axis=0)
            return carry

        lax.fori_loop(0, slots, one, 0)

    def split_block(par, index):
        for t in range(row_tiles):
            value = blocks[par, index, :, t * TILE : (t + 1) * TILE] * scale[...]
            high = value.astype(jnp.bfloat16)
            low = (value - high.astype(jnp.float32)).astype(jnp.bfloat16)
            sources[index * row_tiles + t] = jnp.concatenate([high, low], axis=0)

    def multiply(group):
        totals = [acc[t] for t in range(row_tiles)]
        for slot in range(slots):
            col = cols_smem[group, slot]
            row = rows_smem[group, slot]
            source = sources[group * group_tiles + col]
            product = jnp.dot(
                jnp.concatenate([source, source], axis=1),
                weights[group * slots + slot],
                preferred_element_type=jnp.float32,
            )
            product = product[:vecs] + product[vecs:]
            for t in range(row_tiles):
                totals[t] = totals[t] + jnp.where(row == t, product, 0.0)
        for t in range(row_tiles):
            acc[t] = totals[t]

    def remote(par, index, part, send, recv, target):
        where = blocks.at[par, index] if part is None else blocks.at[par, index, halves[part]]
        return pltpu.make_async_remote_copy(
            src_ref=where, dst_ref=where, send_sem=send, recv_sem=recv,
            device_id=target, device_id_type=pl.DeviceIdType.MESH,
        )

    to_core = {"blk": blk_c}
    to_y = {"blk": blk_y}

    def to_x(step):
        return {"reader": lax.rem(x + step, n_reader)}

    steps = range(1, n_reader)

    def sum_copy(turn, step):
        return pltpu.make_async_remote_copy(
            src_ref=partial_sum.at[turn], dst_ref=sums.at[turn, step - 1],
            send_sem=send_sum.at[turn, step - 1], recv_sem=recv_sum.at[turn, step - 1],
            device_id=peer(step), device_id_type=pl.DeviceIdType.MESH,
        )

    diagonal = (
        lax.broadcasted_iota(jnp.int32, (vecs, TILE), 0)
        == lax.broadcasted_iota(jnp.int32, (vecs, TILE), 1)
    )

    def share_sums(turn, squares):
        own = jnp.sum(squares, axis=1, keepdims=True)
        line = jnp.sum(jnp.where(diagonal, own, 0.0), axis=0, keepdims=True)
        partial_sum[turn] = jnp.broadcast_to(line, partial_sum.shape[1:])
        for step in range(1, peers + 1):
            sum_copy(turn, step).start()

    def norms(turn):
        for step in range(1, peers + 1):
            sum_copy(turn, step).wait()
        total = partial_sum[turn]
        for step in range(1, peers + 1):
            total = total + sums[turn, step - 1]
        spread = jnp.broadcast_to(total[:1], (vecs, TILE))
        squares = jnp.sum(jnp.where(diagonal, spread, 0.0), axis=1, keepdims=True)
        root = jnp.sqrt(squares / total_cols + 1e-06)
        return jnp.broadcast_to(1.0 / root, (vecs, TILE))

    def apply(k, carry):
        par = lax.rem(k, 2)
        x_own = [[remote(par, me, h, send_x.at[s - 1, h], recv_x.at[par, s - 1, h], to_x(s))
                  for h in range(2)] for s in steps]
        y_own = [remote(par, me, h, send_y.at[h], recv_y.at[par, h], to_y) for h in range(2)]
        c_own = remote(par, me, None, send_own, recv_own.at[par], to_core)
        x_block = [block_of(blk, s) for s in steps]
        y_block = block_of(blk_y)
        d_block = [block_of(blk_y, s) for s in steps]
        dy = [remote(par, x_block[s - 1], 0, send_dy.at[s - 1], recv_dy.at[par, s - 1], to_y)
              for s in steps]
        dx = [remote(par, y_block, 1, send_dx.at[s - 1], recv_dx.at[par, s - 1], to_x(s))
              for s in steps]
        cx = [[remote(par, x_block[s - 1], h, send_cx.at[s - 1, h],
                      recv_cx.at[par, s - 1, h], to_core) for h in range(2)] for s in steps]
        cy = [remote(par, y_block, h, send_cy.at[h], recv_cy.at[par, h], to_core)
              for h in range(2)]
        cdy = [remote(par, d_block[s - 1], 0, send_cdy.at[s - 1], recv_cdy.at[par, s - 1],
                      to_core) for s in steps]
        cdx = [remote(par, d_block[s - 1], 1, send_cdx.at[s - 1], recv_cdx.at[par, s - 1],
                      to_core) for s in steps]

        for s in steps:
            x_own[s - 1][0].start()
        y_own[1].start()
        c_own.start()
        for s in steps:
            x_own[s - 1][1].start()
        y_own[0].start()

        acc[...] = jnp.zeros_like(acc)

        @pl.when(k == 0)
        def _():
            split_tiles(blk)
            split_tiles(blk_c)

        @pl.when(k == DEGREE)
        def _():
            scale[...] = norms(0)

        @pl.when(k == DEGREE + 1)
        def _():
            scale[...] = jnp.ones_like(scale)

        split_block(par, me)
        for s in steps:
            x_own[s - 1][0].wait_recv()
            dy[s - 1].start()
            cx[s - 1][0].start()
        y_own[1].wait_recv()
        for s in steps:
            dx[s - 1].start()
        cy[1].start()
        for s in steps:
            x_own[s - 1][1].wait_recv()
            cx[s - 1][1].start()
            split_block(par, x_block[s - 1])
        y_own[0].wait_recv()
        cy[0].start()
        split_block(par, y_block)
        c_own.wait_recv()
        split_block(par, block_of(blk_c))
        multiply(blk)
        for s in steps:
            cx[s - 1][0].wait_recv()
            cx[s - 1][1].wait_recv()
            split_block(par, block_of(blk_c, s))
        multiply(blk_c)

        @pl.when(k == 0)
        def _():
            split_tiles(blk_y)
            split_tiles(blk_yc)

        for s in steps:
            dy[s - 1].wait_recv()
            cdy[s - 1].start()
            dx[s - 1].wait_recv()
            cdx[s - 1].start()
            split_block(par, d_block[s - 1])
        multiply(blk_y)
        cy[1].wait_recv()
        cy[0].wait_recv()
        split_block(par, block_of(blk_yc))
        for s in steps:
            cdy[s - 1].wait_recv()
            cdx[s - 1].wait_recv()
            split_block(par, block_of(blk_yc, s))
        multiply(blk_yc)

        first = lax.rem(k, DEGREE) == 0
        center = center_ref[0]
        gain = jnp.where(first, 1.0, 2.0) / half_ref[0]
        squares = jnp.zeros((vecs, TILE), jnp.float32)
        for t in range(row_tiles):
            lanes = slice(t * TILE, (t + 1) * TILE)
            field = blocks[par, me, :, lanes] * scale[...]
            new = (acc[t] - center * field) * gain
            new = new - jnp.where(first, 0.0, before[:, lanes])
            before[:, lanes] = field
            blocks[1 - par, me, :, lanes] = new
            squares = squares + new * new

        @pl.when(lax.rem(k, DEGREE) == DEGREE - 1)
        def _():
            share_sums(k // DEGREE, squares)

        c_own.wait_send()
        for h in range(2):
            y_own[h].wait_send()
            cy[h].wait_send()
        for s in steps:
            for h in range(2):
                x_own[s - 1][h].wait_send()
                cx[s - 1][h].wait_send()
            for copy in (dx, dy, cdx, cdy):
                copy[s - 1].wait_send()
        return carry

    lax.fori_loop(0, PASSES * DEGREE, apply, 0)
    last = norms(PASSES - 1)
    for t in range(row_tiles):
        lanes = slice(t * TILE, (t + 1) * TILE)
        out_ref[:, lanes] = blocks[PASSES * DEGREE % 2, me, :, lanes] * last


def shards(n_blk, n_reader, vectors, ham_tiles, tile_rows, tile_cols, center, halfwidth):
    vecs, width = vectors.shape
    row_tiles = width // TILE
    n = n_blk * n_reader
    groups, slots = tile_rows.shape[1:]
    others = n_reader - 1
    dma = pltpu.SemaphoreType.DMA
    smem = pl.BlockSpec(memory_space=pltpu.SMEM)
    hbm = pl.BlockSpec(memory_space=pl.ANY)
    vmem = pl.BlockSpec(memory_space=pltpu.VMEM)
    body = functools.partial(kernel, n_blk, n_reader, n * width)
    return pl.pallas_call(
        body,
        out_shape=jax.ShapeDtypeStruct((vecs, width), jnp.float32),
        in_specs=[hbm, hbm, hbm, hbm, smem, smem],
        out_specs=vmem,
        scratch_shapes=[
            pltpu.VMEM((2, n, vecs, width), jnp.float32),
            pltpu.VMEM((n * row_tiles, 2 * vecs, TILE), jnp.bfloat16),
            pltpu.VMEM((groups, slots, TILE, TILE), jnp.float32),
            pltpu.VMEM((groups * slots, 2 * TILE, TILE), jnp.bfloat16),
            pltpu.VMEM((row_tiles, vecs, TILE), jnp.float32),
            pltpu.VMEM((vecs, width), jnp.float32),
            pltpu.VMEM((vecs, TILE), jnp.float32),
            pltpu.VMEM((PASSES, n - 1, 8, TILE), jnp.float32),
            pltpu.VMEM((PASSES, 8, TILE), jnp.float32),
            pltpu.SMEM((groups, slots), jnp.int32),
            pltpu.SMEM((groups, slots), jnp.int32),
            dma((groups,)), dma((3,)),
            dma((others, 2)), dma((2,)), dma((others,)), dma((others,)), dma,
            dma((others, 2)), dma((2,)), dma((others,)), dma((others,)),
            dma((2, others, 2)), dma((2, 2)), dma((2, others)), dma((2, others)), dma((2,)),
            dma((2, others, 2)), dma((2, 2)), dma((2, others)), dma((2, others)),
            dma((PASSES, n - 1)), dma((PASSES, n - 1)),
        ],
        compiler_params=pltpu.CompilerParams(
            collective_id=0, has_side_effects=True, vmem_limit_bytes=56 * 2**20
        ),
        cost_estimate=pl.CostEstimate(
            flops=PASSES * DEGREE * groups * slots * 8 * vecs * TILE * TILE,
            bytes_accessed=groups * slots * TILE * TILE * 4,
            transcendentals=0,
        ),
    )(vectors, ham_tiles, tile_rows, tile_cols, center, halfwidth)


def solution(mesh):
    n_blk, n_reader = mesh.shape["blk"], mesh.shape["reader"]
    return jax.shard_map(
        functools.partial(shards, n_blk, n_reader),
        mesh=mesh,
        in_specs=(
            P("bulk", ("blk", "reader")),
            P(("blk", "reader"), None, None, None, None),
            P(("blk", "reader"), None, None),
            P(("blk", "reader"), None, None),
            P(),
            P(),
        ),
        out_specs=P("bulk", ("blk", "reader")),
        check_vma=False,
    )
```

```python
import functools

import jax
import jax.numpy as jnp
from jax import lax
from jax.experimental import pallas as pl
from jax.experimental.pallas import tpu as pltpu
from jax.sharding import PartitionSpec as P

TILE = 128
PASSES = 2
DEGREE = 3
CORES = 2
STREAMS = 2


def kernel(
    n_blk, n_reader, total_cols,
    vec_ref, ham_ref, rows_ref, cols_ref, center_ref, half_ref,
    out_ref,
    blocks, sources, staged, weights, acc, before, scale, sums, partial_sum,
    rows_smem, cols_smem, ham_sem, in_sem,
    send_x, send_y, send_dx, send_dy, send_own, send_cx, send_cy, send_cdx, send_cdy,
    recv_x, recv_y, recv_dx, recv_dy, recv_own, recv_cx, recv_cy, recv_cdx, recv_cdy,
    send_sum, recv_sum,
):
    vecs = vec_ref.shape[0] // STREAMS
    row_tiles = vec_ref.shape[1] // TILE
    slots = rows_ref.shape[2]
    group_tiles = n_reader * row_tiles
    peers = n_blk * n_reader - 1
    half = vec_ref.shape[1] // 2
    halves = (pl.ds(0, half), pl.ds(half, half))

    blk = lax.axis_index("blk")
    x = lax.axis_index("reader")
    core = lax.rem(blk, CORES)
    side = blk - core
    blk_c = side + (1 - core)
    blk_y = lax.rem(blk + CORES, n_blk)
    blk_yc = lax.rem(blk_c + CORES, n_blk)
    me = blk * n_reader + x

    def peer(step):
        other = lax.rem(me + step, n_blk * n_reader)
        return {"blk": other // n_reader, "reader": lax.rem(other, n_reader)}

    def block_of(b, step=0):
        return b * n_reader + lax.rem(x + n_reader - step, n_reader)

    barrier = pltpu.get_barrier_semaphore()
    for step in range(1, peers + 1):
        pl.semaphore_signal(
            barrier, inc=1, device_id=peer(step), device_id_type=pl.DeviceIdType.MESH
        )

    def ham_copy(group):
        return pltpu.make_async_copy(
            ham_ref.at[0, group], staged.at[group], ham_sem.at[group]
        )

    loads = [
        *(pltpu.make_async_copy(vec_ref.at[pl.ds(st * vecs, vecs)], blocks.at[0, st, me],
                                in_sem.at[2 + st]) for st in range(STREAMS)),
        pltpu.make_async_copy(rows_ref.at[0], rows_smem, in_sem.at[0]),
        pltpu.make_async_copy(cols_ref.at[0], cols_smem, in_sem.at[1]),
    ]
    for copy in loads:
        copy.start()
    for group in (blk, blk_c, blk_y, blk_yc):
        ham_copy(group).start()
    scale[...] = jnp.ones_like(scale)
    before[...] = jnp.zeros_like(before)
    for copy in loads:
        copy.wait()
    pl.semaphore_wait(barrier, peers)

    def split_tiles(group):
        ham_copy(group).wait()

        def one(slot, carry):
            tile = staged[group, slot].T
            high = tile.astype(jnp.bfloat16)
            low = (tile - high.astype(jnp.float32)).astype(jnp.bfloat16)
            weights[group * slots + slot] = jnp.concatenate([high, low], axis=0)
            return carry

        lax.fori_loop(0, slots, one, 0)

    def split_block(st, par, index):
        for t in range(row_tiles):
            value = blocks[par, st, index, :, t * TILE : (t + 1) * TILE] * scale[st]
            high = value.astype(jnp.bfloat16).astype(jnp.float32)
            both = jnp.concatenate([high, value - high], axis=0)
            sources[st, index * row_tiles + t] = both.astype(jnp.bfloat16)

    def multiply(st, group):
        totals = [acc[st, t] for t in range(row_tiles)]
        for slot in range(slots):
            col = cols_smem[group, slot]
            row = rows_smem[group, slot]
            source = sources[st, group * group_tiles + col]
            product = jnp.dot(
                jnp.concatenate([source, source], axis=1),
                weights[group * slots + slot],
                preferred_element_type=jnp.float32,
            )
            product = product[:vecs] + product[vecs:]
            for t in range(row_tiles):
                totals[t] = totals[t] + jnp.where(row == t, product, 0.0)
        for t in range(row_tiles):
            acc[st, t] = totals[t]

    to_core = {"blk": blk_c}
    to_y = {"blk": blk_y}

    def to_x(step):
        return {"reader": lax.rem(x + step, n_reader)}

    steps = range(1, n_reader)
    x_block = [block_of(blk, s) for s in steps]
    y_block = block_of(blk_y)
    d_block = [block_of(blk_y, s) for s in steps]

    def copies(st, k):
        par = lax.rem(k, 2)

        def remote(index, part, send, recv, target):
            where = blocks.at[par, st, index]
            if part is not None:
                where = blocks.at[par, st, index, :, halves[part]]
            return pltpu.make_async_remote_copy(
                src_ref=where, dst_ref=where, send_sem=send, recv_sem=recv,
                device_id=target, device_id_type=pl.DeviceIdType.MESH,
            )

        return dict(
            x=[[remote(me, h, send_x.at[st, s - 1, h], recv_x.at[st, par, s - 1, h], to_x(s))
                for h in range(2)] for s in steps],
            y=[remote(me, h, send_y.at[st, h], recv_y.at[st, par, h], to_y) for h in range(2)],
            own=remote(me, None, send_own.at[st], recv_own.at[st, par], to_core),
            dy=[remote(x_block[s - 1], 0, send_dy.at[st, s - 1], recv_dy.at[st, par, s - 1],
                       to_y) for s in steps],
            dx=[remote(y_block, 1, send_dx.at[st, s - 1], recv_dx.at[st, par, s - 1], to_x(s))
                for s in steps],
            cx=[[remote(x_block[s - 1], h, send_cx.at[st, s - 1, h],
                        recv_cx.at[st, par, s - 1, h], to_core) for h in range(2)]
                for s in steps],
            cy=[remote(y_block, h, send_cy.at[st, h], recv_cy.at[st, par, h], to_core)
                for h in range(2)],
            cdy=[remote(d_block[s - 1], 0, send_cdy.at[st, s - 1], recv_cdy.at[st, par, s - 1],
                        to_core) for s in steps],
            cdx=[remote(d_block[s - 1], 1, send_cdx.at[st, s - 1], recv_cdx.at[st, par, s - 1],
                        to_core) for s in steps],
        )

    def sum_copy(st, turn, step):
        at = turn * STREAMS + st
        return pltpu.make_async_remote_copy(
            src_ref=partial_sum.at[at], dst_ref=sums.at[at, step - 1],
            send_sem=send_sum.at[at, step - 1], recv_sem=recv_sum.at[at, step - 1],
            device_id=peer(step), device_id_type=pl.DeviceIdType.MESH,
        )

    diagonal = (
        lax.broadcasted_iota(jnp.int32, (vecs, TILE), 0)
        == lax.broadcasted_iota(jnp.int32, (vecs, TILE), 1)
    )

    def share_sums(st, turn, squares):
        own = jnp.sum(squares, axis=1, keepdims=True)
        line = jnp.sum(jnp.where(diagonal, own, 0.0), axis=0, keepdims=True)
        partial_sum[turn * STREAMS + st] = jnp.broadcast_to(line, partial_sum.shape[1:])
        for step in range(1, peers + 1):
            sum_copy(st, turn, step).start()

    def norms(st, turn):
        for step in range(1, peers + 1):
            sum_copy(st, turn, step).wait()
        total = partial_sum[turn * STREAMS + st]
        for step in range(1, peers + 1):
            total = total + sums[turn * STREAMS + st, step - 1]
        spread = jnp.broadcast_to(total[:1], (vecs, TILE))
        squares = jnp.sum(jnp.where(diagonal, spread, 0.0), axis=1, keepdims=True)
        root = jnp.sqrt(squares / total_cols + 1e-06)
        return jnp.broadcast_to(1.0 / root, (vecs, TILE))

    def send(st, k):
        c = copies(st, k)
        for s in steps:
            c["x"][s - 1][0].start()
        c["y"][1].start()
        c["own"].start()
        for s in steps:
            c["x"][s - 1][1].start()
        c["y"][0].start()

    def pass_on(st, k):
        par = lax.rem(k, 2)
        c = copies(st, k)
        for s in steps:
            c["x"][s - 1][0].wait_recv()
            c["dy"][s - 1].start()
            c["cx"][s - 1][0].start()
        c["y"][1].wait_recv()
        for s in steps:
            c["dx"][s - 1].start()
        c["cy"][1].start()
        for s in steps:
            c["x"][s - 1][1].wait_recv()
            c["cx"][s - 1][1].start()
        c["y"][0].wait_recv()
        c["cy"][0].start()

        @pl.when(k == DEGREE)
        def _():
            scale[st] = norms(st, 0)

        @pl.when(k == DEGREE + 1)
        def _():
            scale[st] = jnp.ones_like(scale[st])

        split_block(st, par, me)
        for s in steps:
            split_block(st, par, x_block[s - 1])
        split_block(st, par, y_block)

    def near(st, k):
        par = lax.rem(k, 2)
        c = copies(st, k)
        acc[st] = jnp.zeros_like(acc[st])
        multiply(st, blk)
        c["own"].wait_recv()
        split_block(st, par, block_of(blk_c))
        for s in steps:
            for h in range(2):
                c["cx"][s - 1][h].wait_recv()
            split_block(st, par, block_of(blk_c, s))
        multiply(st, blk_c)

    def corner(st, k):
        par = lax.rem(k, 2)
        c = copies(st, k)
        for s in steps:
            c["dy"][s - 1].wait_recv()
            c["cdy"][s - 1].start()
            c["dx"][s - 1].wait_recv()
            c["cdx"][s - 1].start()
            split_block(st, par, d_block[s - 1])

    def far(st, k):
        par = lax.rem(k, 2)
        c = copies(st, k)
        multiply(st, blk_y)
        for h in range(2):
            c["cy"][h].wait_recv()
        split_block(st, par, block_of(blk_yc))
        for s in steps:
            c["cdy"][s - 1].wait_recv()
            c["cdx"][s - 1].wait_recv()
            split_block(st, par, block_of(blk_yc, s))
        multiply(st, blk_yc)

        first = lax.rem(k, DEGREE) == 0
        center = center_ref[0]
        gain = jnp.where(first, 1.0, 2.0) / half_ref[0]
        squares = jnp.zeros((vecs, TILE), jnp.float32)
        for t in range(row_tiles):
            lanes = slice(t * TILE, (t + 1) * TILE)
            field = blocks[par, st, me, :, lanes] * scale[st]
            new = (acc[st, t] - center * field) * gain
            new = new - jnp.where(first, 0.0, before[st, :, lanes])
            before[st, :, lanes] = field
            blocks[1 - par, st, me, :, lanes] = new
            squares = squares + new * new

        @pl.when(lax.rem(k, DEGREE) == DEGREE - 1)
        def _():
            share_sums(st, k // DEGREE, squares)

        c["own"].wait_send()
        for h in range(2):
            c["y"][h].wait_send()
            c["cy"][h].wait_send()
        for s in steps:
            for h in range(2):
                c["x"][s - 1][h].wait_send()
                c["cx"][s - 1][h].wait_send()
            for name in ("dx", "dy", "cdx", "cdy"):
                c[name][s - 1].wait_send()

        @pl.when(k + 1 < total_steps)
        def _():
            send(st, k + 1)

    total_steps = PASSES * DEGREE
    send(0, 0)
    send(1, 0)
    split_tiles(blk)
    split_tiles(blk_c)
    pass_on(0, 0)
    split_tiles(blk_y)
    split_tiles(blk_yc)

    def apply(k, carry):
        near(0, k)
        pass_on(1, k)
        corner(0, k)
        far(0, k)
        near(1, k)
        corner(1, k)

        @pl.when(k + 1 < total_steps)
        def _():
            pass_on(0, k + 1)

        far(1, k)
        return carry

    lax.fori_loop(0, total_steps, apply, 0)
    for st in range(STREAMS):
        last = norms(st, PASSES - 1)
        for t in range(row_tiles):
            lanes = slice(t * TILE, (t + 1) * TILE)
            out_ref[st * vecs : (st + 1) * vecs, lanes] = (
                blocks[total_steps % 2, st, me, :, lanes] * last
            )


def shards(n_blk, n_reader, vectors, ham_tiles, tile_rows, tile_cols, center, halfwidth):
    vecs, width = vectors.shape
    row_tiles = width // TILE
    n = n_blk * n_reader
    groups, slots = tile_rows.shape[1:]
    others = n_reader - 1
    q = STREAMS
    part = vecs // STREAMS
    dma = pltpu.SemaphoreType.DMA
    smem = pl.BlockSpec(memory_space=pltpu.SMEM)
    hbm = pl.BlockSpec(memory_space=pl.ANY)
    vmem = pl.BlockSpec(memory_space=pltpu.VMEM)
    body = functools.partial(kernel, n_blk, n_reader, n * width)
    return pl.pallas_call(
        body,
        out_shape=jax.ShapeDtypeStruct((vecs, width), jnp.float32),
        in_specs=[hbm, hbm, hbm, hbm, smem, smem],
        out_specs=vmem,
        scratch_shapes=[
            pltpu.VMEM((2, STREAMS, n, part, width), jnp.float32),
            pltpu.VMEM((STREAMS, n * row_tiles, 2 * part, TILE), jnp.bfloat16),
            pltpu.VMEM((groups, slots, TILE, TILE), jnp.float32),
            pltpu.VMEM((groups * slots, 2 * TILE, TILE), jnp.bfloat16),
            pltpu.VMEM((STREAMS, row_tiles, part, TILE), jnp.float32),
            pltpu.VMEM((STREAMS, part, width), jnp.float32),
            pltpu.VMEM((STREAMS, part, TILE), jnp.float32),
            pltpu.VMEM((PASSES * STREAMS, n - 1, 8, TILE), jnp.float32),
            pltpu.VMEM((PASSES * STREAMS, 8, TILE), jnp.float32),
            pltpu.SMEM((groups, slots), jnp.int32),
            pltpu.SMEM((groups, slots), jnp.int32),
            dma((groups,)), dma((4,)),
            dma((q, others, 2)), dma((q, 2)), dma((q, others)), dma((q, others)), dma((q,)),
            dma((q, others, 2)), dma((q, 2)), dma((q, others)), dma((q, others)),
            dma((q, 2, others, 2)), dma((q, 2, 2)), dma((q, 2, others)), dma((q, 2, others)),
            dma((q, 2)),
            dma((q, 2, others, 2)), dma((q, 2, 2)), dma((q, 2, others)), dma((q, 2, others)),
            dma((PASSES * q, n - 1)), dma((PASSES * q, n - 1)),
        ],
        compiler_params=pltpu.CompilerParams(
            collective_id=0, has_side_effects=True, vmem_limit_bytes=56 * 2**20
        ),
        cost_estimate=pl.CostEstimate(
            flops=PASSES * DEGREE * groups * slots * 8 * vecs * TILE * TILE,
            bytes_accessed=groups * slots * TILE * TILE * 4,
            transcendentals=0,
        ),
    )(vectors, ham_tiles, tile_rows, tile_cols, center, halfwidth)


def solution(mesh):
    n_blk, n_reader = mesh.shape["blk"], mesh.shape["reader"]
    return jax.shard_map(
        functools.partial(shards, n_blk, n_reader),
        mesh=mesh,
        in_specs=(
            P("bulk", ("blk", "reader")),
            P(("blk", "reader"), None, None, None, None),
            P(("blk", "reader"), None, None),
            P(("blk", "reader"), None, None),
            P(),
            P(),
        ),
        out_specs=P("bulk", ("blk", "reader")),
        check_vma=False,
    )
```

```python
import functools

import jax
import jax.numpy as jnp
from jax import lax
from jax.experimental import pallas as pl
from jax.experimental.pallas import tpu as pltpu
from jax.sharding import PartitionSpec as P

TILE = 128
PASSES = 2
DEGREE = 3
CORES = 2


def kernel(
    n_blk, n_reader, total_cols,
    vec_ref, ham_ref, rows_ref, cols_ref, center_ref, half_ref,
    out_ref,
    blocks, sources, staged, weights, acc, before, scale, sums, partial_sum,
    rows_smem, cols_smem, ham_sem, in_sem,
    send_x, send_y, send_dx, send_dy, send_own, send_cx, send_cy, send_cdx, send_cdy,
    recv_x, recv_y, recv_dx, recv_dy, recv_own, recv_cx, recv_cy, recv_cdx, recv_cdy,
    send_sum, recv_sum,
):
    vecs = vec_ref.shape[0]
    row_tiles = vec_ref.shape[1] // TILE
    slots = rows_ref.shape[2]
    group_tiles = n_reader * row_tiles
    peers = n_blk * n_reader - 1
    half = vecs // 2
    halves = (pl.ds(0, half), pl.ds(half, half))

    blk = lax.axis_index("blk")
    x = lax.axis_index("reader")
    core = lax.rem(blk, CORES)
    side = blk - core
    blk_c = side + (1 - core)
    blk_y = lax.rem(blk + CORES, n_blk)
    blk_yc = lax.rem(blk_c + CORES, n_blk)
    me = blk * n_reader + x

    def peer(step):
        other = lax.rem(me + step, n_blk * n_reader)
        return {"blk": other // n_reader, "reader": lax.rem(other, n_reader)}

    def block_of(b, step=0):
        return b * n_reader + lax.rem(x + n_reader - step, n_reader)

    barrier = pltpu.get_barrier_semaphore()
    for step in range(1, peers + 1):
        pl.semaphore_signal(
            barrier, inc=1, device_id=peer(step), device_id_type=pl.DeviceIdType.MESH
        )

    def ham_copy(group):
        return pltpu.make_async_copy(
            ham_ref.at[0, group], staged.at[group], ham_sem.at[group]
        )

    loads = [
        pltpu.make_async_copy(vec_ref, blocks.at[0, me], in_sem.at[0]),
        pltpu.make_async_copy(rows_ref.at[0], rows_smem, in_sem.at[1]),
        pltpu.make_async_copy(cols_ref.at[0], cols_smem, in_sem.at[2]),
    ]
    for copy in loads:
        copy.start()
    for group in (blk, blk_c, blk_y, blk_yc):
        ham_copy(group).start()
    scale[...] = jnp.ones_like(scale)
    before[...] = jnp.zeros_like(before)
    for copy in loads:
        copy.wait()
    pl.semaphore_wait(barrier, peers)

    def split_tiles(group):
        ham_copy(group).wait()

        def one(slot, carry):
            tile = staged[group, slot].T
            high = tile.astype(jnp.bfloat16)
            low = (tile - high.astype(jnp.float32)).astype(jnp.bfloat16)
            weights[group * slots + slot] = jnp.concatenate([high, low], axis=1)
            return carry

        lax.fori_loop(0, slots, one, 0)

    def split_block(par, index):
        for t in range(row_tiles):
            value = blocks[par, index, :, t * TILE : (t + 1) * TILE] * scale[...]
            high = value.astype(jnp.bfloat16)
            low = (value - high.astype(jnp.float32)).astype(jnp.bfloat16)
            sources[index * row_tiles + t] = jnp.concatenate([high, low], axis=0)

    def multiply(group):
        totals = [acc[t] for t in range(row_tiles)]
        for slot in range(slots):
            col = cols_smem[group, slot]
            row = rows_smem[group, slot]
            source = sources[group * group_tiles + col]
            product = jnp.dot(
                source,
                weights[group * slots + slot],
                preferred_element_type=jnp.float32,
            )
            product = product[:vecs, :TILE] + (product[vecs:, :TILE] + product[:vecs, TILE:])
            for t in range(row_tiles):
                totals[t] = totals[t] + jnp.where(row == t, product, 0.0)
        for t in range(row_tiles):
            acc[t] = totals[t]

    def remote(par, index, part, send, recv, target):
        where = blocks.at[par, index] if part is None else blocks.at[par, index, halves[part]]
        return pltpu.make_async_remote_copy(
            src_ref=where, dst_ref=where, send_sem=send, recv_sem=recv,
            device_id=target, device_id_type=pl.DeviceIdType.MESH,
        )

    to_core = {"blk": blk_c}
    to_y = {"blk": blk_y}

    def to_x(step):
        return {"reader": lax.rem(x + step, n_reader)}

    steps = range(1, n_reader)

    def sum_copy(turn, step):
        return pltpu.make_async_remote_copy(
            src_ref=partial_sum.at[turn], dst_ref=sums.at[turn, step - 1],
            send_sem=send_sum.at[turn, step - 1], recv_sem=recv_sum.at[turn, step - 1],
            device_id=peer(step), device_id_type=pl.DeviceIdType.MESH,
        )

    diagonal = (
        lax.broadcasted_iota(jnp.int32, (vecs, TILE), 0)
        == lax.broadcasted_iota(jnp.int32, (vecs, TILE), 1)
    )

    def share_sums(turn, squares):
        own = jnp.sum(squares, axis=1, keepdims=True)
        line = jnp.sum(jnp.where(diagonal, own, 0.0), axis=0, keepdims=True)
        partial_sum[turn] = jnp.broadcast_to(line, partial_sum.shape[1:])
        for step in range(1, peers + 1):
            sum_copy(turn, step).start()

    def norms(turn):
        for step in range(1, peers + 1):
            sum_copy(turn, step).wait()
        total = partial_sum[turn]
        for step in range(1, peers + 1):
            total = total + sums[turn, step - 1]
        spread = jnp.broadcast_to(total[:1], (vecs, TILE))
        squares = jnp.sum(jnp.where(diagonal, spread, 0.0), axis=1, keepdims=True)
        root = jnp.sqrt(squares / total_cols + 1e-06)
        return jnp.broadcast_to(1.0 / root, (vecs, TILE))

    def apply(k, carry):
        par = lax.rem(k, 2)
        x_own = [[remote(par, me, h, send_x.at[s - 1, h], recv_x.at[par, s - 1, h], to_x(s))
                  for h in range(2)] for s in steps]
        y_own = [remote(par, me, h, send_y.at[h], recv_y.at[par, h], to_y) for h in range(2)]
        c_own = remote(par, me, None, send_own, recv_own.at[par], to_core)
        x_block = [block_of(blk, s) for s in steps]
        y_block = block_of(blk_y)
        d_block = [block_of(blk_y, s) for s in steps]
        dy = [remote(par, x_block[s - 1], 0, send_dy.at[s - 1], recv_dy.at[par, s - 1], to_y)
              for s in steps]
        dx = [remote(par, y_block, 1, send_dx.at[s - 1], recv_dx.at[par, s - 1], to_x(s))
              for s in steps]
        cx = [[remote(par, x_block[s - 1], h, send_cx.at[s - 1, h],
                      recv_cx.at[par, s - 1, h], to_core) for h in range(2)] for s in steps]
        cy = [remote(par, y_block, h, send_cy.at[h], recv_cy.at[par, h], to_core)
              for h in range(2)]
        cdy = [remote(par, d_block[s - 1], 0, send_cdy.at[s - 1], recv_cdy.at[par, s - 1],
                      to_core) for s in steps]
        cdx = [remote(par, d_block[s - 1], 1, send_cdx.at[s - 1], recv_cdx.at[par, s - 1],
                      to_core) for s in steps]

        for s in steps:
            x_own[s - 1][0].start()
        y_own[1].start()
        c_own.start()
        for s in steps:
            x_own[s - 1][1].start()
        y_own[0].start()

        acc[...] = jnp.zeros_like(acc)

        @pl.when(k == 0)
        def _():
            split_tiles(blk)
            split_tiles(blk_c)

        @pl.when(k == DEGREE)
        def _():
            scale[...] = norms(0)

        @pl.when(k == DEGREE + 1)
        def _():
            scale[...] = jnp.ones_like(scale)

        split_block(par, me)
        for s in steps:
            x_own[s - 1][0].wait_recv()
            dy[s - 1].start()
            cx[s - 1][0].start()
        y_own[1].wait_recv()
        for s in steps:
            dx[s - 1].start()
        cy[1].start()
        for s in steps:
            x_own[s - 1][1].wait_recv()
            cx[s - 1][1].start()
            split_block(par, x_block[s - 1])
        y_own[0].wait_recv()
        cy[0].start()
        split_block(par, y_block)
        c_own.wait_recv()
        split_block(par, block_of(blk_c))
        multiply(blk)
        for s in steps:
            cx[s - 1][0].wait_recv()
            cx[s - 1][1].wait_recv()
            split_block(par, block_of(blk_c, s))
        multiply(blk_c)

        @pl.when(k == 0)
        def _():
            split_tiles(blk_y)
            split_tiles(blk_yc)

        for s in steps:
            dy[s - 1].wait_recv()
            cdy[s - 1].start()
            dx[s - 1].wait_recv()
            cdx[s - 1].start()
            split_block(par, d_block[s - 1])
        multiply(blk_y)
        cy[1].wait_recv()
        cy[0].wait_recv()
        split_block(par, block_of(blk_yc))
        for s in steps:
            cdy[s - 1].wait_recv()
            cdx[s - 1].wait_recv()
            split_block(par, block_of(blk_yc, s))
        multiply(blk_yc)

        first = lax.rem(k, DEGREE) == 0
        center = center_ref[0]
        gain = jnp.where(first, 1.0, 2.0) / half_ref[0]
        squares = jnp.zeros((vecs, TILE), jnp.float32)
        for t in range(row_tiles):
            lanes = slice(t * TILE, (t + 1) * TILE)
            field = blocks[par, me, :, lanes] * scale[...]
            new = (acc[t] - center * field) * gain
            new = new - jnp.where(first, 0.0, before[:, lanes])
            before[:, lanes] = field
            blocks[1 - par, me, :, lanes] = new
            squares = squares + new * new

        @pl.when(lax.rem(k, DEGREE) == DEGREE - 1)
        def _():
            share_sums(k // DEGREE, squares)

        c_own.wait_send()
        for h in range(2):
            y_own[h].wait_send()
            cy[h].wait_send()
        for s in steps:
            for h in range(2):
                x_own[s - 1][h].wait_send()
                cx[s - 1][h].wait_send()
            for copy in (dx, dy, cdx, cdy):
                copy[s - 1].wait_send()
        return carry

    lax.fori_loop(0, PASSES * DEGREE, apply, 0)
    last = norms(PASSES - 1)
    for t in range(row_tiles):
        lanes = slice(t * TILE, (t + 1) * TILE)
        out_ref[:, lanes] = blocks[PASSES * DEGREE % 2, me, :, lanes] * last


def shards(n_blk, n_reader, vectors, ham_tiles, tile_rows, tile_cols, center, halfwidth):
    vecs, width = vectors.shape
    row_tiles = width // TILE
    n = n_blk * n_reader
    groups, slots = tile_rows.shape[1:]
    others = n_reader - 1
    dma = pltpu.SemaphoreType.DMA
    smem = pl.BlockSpec(memory_space=pltpu.SMEM)
    hbm = pl.BlockSpec(memory_space=pl.ANY)
    vmem = pl.BlockSpec(memory_space=pltpu.VMEM)
    body = functools.partial(kernel, n_blk, n_reader, n * width)
    return pl.pallas_call(
        body,
        out_shape=jax.ShapeDtypeStruct((vecs, width), jnp.float32),
        in_specs=[hbm, hbm, hbm, hbm, smem, smem],
        out_specs=vmem,
        scratch_shapes=[
            pltpu.VMEM((2, n, vecs, width), jnp.float32),
            pltpu.VMEM((n * row_tiles, 2 * vecs, TILE), jnp.bfloat16),
            pltpu.VMEM((groups, slots, TILE, TILE), jnp.float32),
            pltpu.VMEM((groups * slots, TILE, 2 * TILE), jnp.bfloat16),
            pltpu.VMEM((row_tiles, vecs, TILE), jnp.float32),
            pltpu.VMEM((vecs, width), jnp.float32),
            pltpu.VMEM((vecs, TILE), jnp.float32),
            pltpu.VMEM((PASSES, n - 1, 8, TILE), jnp.float32),
            pltpu.VMEM((PASSES, 8, TILE), jnp.float32),
            pltpu.SMEM((groups, slots), jnp.int32),
            pltpu.SMEM((groups, slots), jnp.int32),
            dma((groups,)), dma((3,)),
            dma((others, 2)), dma((2,)), dma((others,)), dma((others,)), dma,
            dma((others, 2)), dma((2,)), dma((others,)), dma((others,)),
            dma((2, others, 2)), dma((2, 2)), dma((2, others)), dma((2, others)), dma((2,)),
            dma((2, others, 2)), dma((2, 2)), dma((2, others)), dma((2, others)),
            dma((PASSES, n - 1)), dma((PASSES, n - 1)),
        ],
        compiler_params=pltpu.CompilerParams(
            collective_id=0, has_side_effects=True, vmem_limit_bytes=56 * 2**20
        ),
        cost_estimate=pl.CostEstimate(
            flops=PASSES * DEGREE * groups * slots * 8 * vecs * TILE * TILE,
            bytes_accessed=groups * slots * TILE * TILE * 4,
            transcendentals=0,
        ),
    )(vectors, ham_tiles, tile_rows, tile_cols, center, halfwidth)


def solution(mesh):
    n_blk, n_reader = mesh.shape["blk"], mesh.shape["reader"]
    return jax.shard_map(
        functools.partial(shards, n_blk, n_reader),
        mesh=mesh,
        in_specs=(
            P("bulk", ("blk", "reader")),
            P(("blk", "reader"), None, None, None, None),
            P(("blk", "reader"), None, None),
            P(("blk", "reader"), None, None),
            P(),
            P(),
        ),
        out_specs=P("bulk", ("blk", "reader")),
        check_vma=False,
    )
```

```python
import functools

import jax
import jax.numpy as jnp
from jax import lax
from jax.experimental import pallas as pl
from jax.experimental.pallas import tpu as pltpu
from jax.sharding import PartitionSpec as P

TILE = 128
PASSES = 2
DEGREE = 3
CORES = 2


def kernel(
    n_blk, n_reader, total_cols,
    vec_ref, ham_ref, rows_ref, cols_ref, center_ref, half_ref,
    out_ref,
    blocks, sources, staged, weights, acc, before, scale, sums, partial_sum,
    rows_smem, cols_smem, ham_sem, in_sem,
    send_x, send_y, send_dx, send_dy, send_own, send_cx, send_cy, send_cdx, send_cdy,
    recv_x, recv_y, recv_dx, recv_dy, recv_own, recv_cx, recv_cy, recv_cdx, recv_cdy,
    send_sum, recv_sum,
):
    vecs = vec_ref.shape[0]
    row_tiles = vec_ref.shape[1] // TILE
    slots = rows_ref.shape[2]
    group_tiles = n_reader * row_tiles
    peers = n_blk * n_reader - 1
    half = vecs // 2
    halves = (pl.ds(0, half), pl.ds(half, half))

    blk = lax.axis_index("blk")
    x = lax.axis_index("reader")
    core = lax.rem(blk, CORES)
    side = blk - core
    blk_c = side + (1 - core)
    blk_y = lax.rem(blk + CORES, n_blk)
    blk_yc = lax.rem(blk_c + CORES, n_blk)
    me = blk * n_reader + x

    def peer(step):
        other = lax.rem(me + step, n_blk * n_reader)
        return {"blk": other // n_reader, "reader": lax.rem(other, n_reader)}

    def block_of(b, step=0):
        return b * n_reader + lax.rem(x + n_reader - step, n_reader)

    barrier = pltpu.get_barrier_semaphore()
    for step in range(1, peers + 1):
        pl.semaphore_signal(
            barrier, inc=1, device_id=peer(step), device_id_type=pl.DeviceIdType.MESH
        )

    def ham_copy(group):
        return pltpu.make_async_copy(
            ham_ref.at[0, group], staged.at[group], ham_sem.at[group]
        )

    loads = [
        pltpu.make_async_copy(vec_ref, blocks.at[0, me], in_sem.at[0]),
        pltpu.make_async_copy(rows_ref.at[0], rows_smem, in_sem.at[1]),
        pltpu.make_async_copy(cols_ref.at[0], cols_smem, in_sem.at[2]),
    ]
    for copy in loads:
        copy.start()
    for group in (blk, blk_c, blk_y, blk_yc):
        ham_copy(group).start()
    scale[...] = jnp.ones_like(scale)
    before[...] = jnp.zeros_like(before)
    for copy in loads:
        copy.wait()
    pl.semaphore_wait(barrier, peers)

    def split_tiles(group):
        ham_copy(group).wait()

        def one(slot, carry):
            tile = staged[group, slot].T
            high = tile.astype(jnp.bfloat16)
            low = (tile - high.astype(jnp.float32)).astype(jnp.bfloat16)
            weights[group * slots + slot] = jnp.concatenate([high, low], axis=0)
            return carry

        lax.fori_loop(0, slots, one, 0)

    def split_block(par, index):
        for t in range(row_tiles):
            value = blocks[par, index, :, t * TILE : (t + 1) * TILE] * scale[...]
            high = value.astype(jnp.bfloat16)
            low = (value - high.astype(jnp.float32)).astype(jnp.bfloat16)
            sources[index * row_tiles + t] = jnp.concatenate([high, low], axis=0)

    def multiply(group):
        totals = [acc[t] for t in range(row_tiles)]
        for slot in range(slots):
            col = cols_smem[group, slot]
            row = rows_smem[group, slot]
            source = sources[group * group_tiles + col]
            product = jnp.dot(
                jnp.concatenate([source, source], axis=1),
                weights[group * slots + slot],
                preferred_element_type=jnp.float32,
            )
            product = product[:vecs] + product[vecs:]
            for t in range(row_tiles):
                totals[t] = totals[t] + jnp.where(row == t, product, 0.0)
        for t in range(row_tiles):
            acc[t] = totals[t]

    def remote(par, index, part, send, recv, target):
        where = blocks.at[par, index] if part is None else blocks.at[par, index, halves[part]]
        return pltpu.make_async_remote_copy(
            src_ref=where, dst_ref=where, send_sem=send, recv_sem=recv,
            device_id=target, device_id_type=pl.DeviceIdType.MESH,
        )

    to_core = {"blk": blk_c}
    to_y = {"blk": blk_y}

    def to_x(step):
        return {"reader": lax.rem(x + step, n_reader)}

    steps = range(1, n_reader)

    def sum_copy(turn, step):
        return pltpu.make_async_remote_copy(
            src_ref=partial_sum.at[turn], dst_ref=sums.at[turn, step - 1],
            send_sem=send_sum.at[turn, step - 1], recv_sem=recv_sum.at[turn, step - 1],
            device_id=peer(step), device_id_type=pl.DeviceIdType.MESH,
        )

    diagonal = (
        lax.broadcasted_iota(jnp.int32, (vecs, TILE), 0)
        == lax.broadcasted_iota(jnp.int32, (vecs, TILE), 1)
    )

    def share_sums(turn, squares):
        own = jnp.sum(squares, axis=1, keepdims=True)
        line = jnp.sum(jnp.where(diagonal, own, 0.0), axis=0, keepdims=True)
        partial_sum[turn] = jnp.broadcast_to(line, partial_sum.shape[1:])
        for step in range(1, peers + 1):
            sum_copy(turn, step).start()

    def norms(turn):
        for step in range(1, peers + 1):
            sum_copy(turn, step).wait()
        total = partial_sum[turn]
        for step in range(1, peers + 1):
            total = total + sums[turn, step - 1]
        spread = jnp.broadcast_to(total[:1], (vecs, TILE))
        squares = jnp.sum(jnp.where(diagonal, spread, 0.0), axis=1, keepdims=True)
        root = jnp.sqrt(squares / total_cols + 1e-06)
        return jnp.broadcast_to(1.0 / root, (vecs, TILE))

    def apply(k, carry):
        par = lax.rem(k, 2)
        x_own = [[remote(par, me, h, send_x.at[s - 1, h], recv_x.at[par, s - 1, h], to_x(s))
                  for h in range(2)] for s in steps]
        y_own = [remote(par, me, h, send_y.at[h], recv_y.at[par, h], to_y) for h in range(2)]
        c_own = remote(par, me, None, send_own, recv_own.at[par], to_core)
        x_block = [block_of(blk, s) for s in steps]
        y_block = block_of(blk_y)
        d_block = [block_of(blk_y, s) for s in steps]
        dy = [remote(par, x_block[s - 1], 0, send_dy.at[s - 1], recv_dy.at[par, s - 1], to_y)
              for s in steps]
        dx = [remote(par, y_block, 1, send_dx.at[s - 1], recv_dx.at[par, s - 1], to_x(s))
              for s in steps]
        cx = [remote(par, x_block[s - 1], None, send_cx.at[s - 1, 0],
                     recv_cx.at[par, s - 1, 0], to_core) for s in steps]
        cy = remote(par, y_block, None, send_cy.at[0], recv_cy.at[par, 0], to_core)
        cdy = [remote(par, d_block[s - 1], 0, send_cdy.at[s - 1], recv_cdy.at[par, s - 1],
                      to_core) for s in steps]
        cdx = [remote(par, d_block[s - 1], 1, send_cdx.at[s - 1], recv_cdx.at[par, s - 1],
                      to_core) for s in steps]

        for s in steps:
            x_own[s - 1][0].start()
        y_own[1].start()
        c_own.start()
        for s in steps:
            x_own[s - 1][1].start()
        y_own[0].start()

        acc[...] = jnp.zeros_like(acc)

        @pl.when(k == 0)
        def _():
            split_tiles(blk)
            split_tiles(blk_c)

        @pl.when(k == DEGREE)
        def _():
            scale[...] = norms(0)

        @pl.when(k == DEGREE + 1)
        def _():
            scale[...] = jnp.ones_like(scale)

        split_block(par, me)
        for s in steps:
            x_own[s - 1][0].wait_recv()
            dy[s - 1].start()
        y_own[1].wait_recv()
        for s in steps:
            dx[s - 1].start()
        for s in steps:
            x_own[s - 1][1].wait_recv()
            cx[s - 1].start()
            split_block(par, x_block[s - 1])
        y_own[0].wait_recv()
        cy.start()
        split_block(par, y_block)
        c_own.wait_recv()
        split_block(par, block_of(blk_c))
        multiply(blk)
        for s in steps:
            cx[s - 1].wait_recv()
            split_block(par, block_of(blk_c, s))
        multiply(blk_c)

        @pl.when(k == 0)
        def _():
            split_tiles(blk_y)
            split_tiles(blk_yc)

        for s in steps:
            dy[s - 1].wait_recv()
            cdy[s - 1].start()
            dx[s - 1].wait_recv()
            cdx[s - 1].start()
            split_block(par, d_block[s - 1])
        multiply(blk_y)
        cy.wait_recv()
        split_block(par, block_of(blk_yc))
        for s in steps:
            cdy[s - 1].wait_recv()
            cdx[s - 1].wait_recv()
            split_block(par, block_of(blk_yc, s))
        multiply(blk_yc)

        first = lax.rem(k, DEGREE) == 0
        center = center_ref[0]
        gain = jnp.where(first, 1.0, 2.0) / half_ref[0]
        squares = jnp.zeros((vecs, TILE), jnp.float32)
        for t in range(row_tiles):
            lanes = slice(t * TILE, (t + 1) * TILE)
            field = blocks[par, me, :, lanes] * scale[...]
            new = (acc[t] - center * field) * gain
            new = new - jnp.where(first, 0.0, before[:, lanes])
            before[:, lanes] = field
            blocks[1 - par, me, :, lanes] = new
            squares = squares + new * new

        @pl.when(lax.rem(k, DEGREE) == DEGREE - 1)
        def _():
            share_sums(k // DEGREE, squares)

        c_own.wait_send()
        for h in range(2):
            y_own[h].wait_send()
        cy.wait_send()
        for s in steps:
            for h in range(2):
                x_own[s - 1][h].wait_send()
            for copy in (dx, dy, cx, cdx, cdy):
                copy[s - 1].wait_send()
        return carry

    lax.fori_loop(0, PASSES * DEGREE, apply, 0)
    last = norms(PASSES - 1)
    for t in range(row_tiles):
        lanes = slice(t * TILE, (t + 1) * TILE)
        out_ref[:, lanes] = blocks[PASSES * DEGREE % 2, me, :, lanes] * last


def shards(n_blk, n_reader, vectors, ham_tiles, tile_rows, tile_cols, center, halfwidth):
    vecs, width = vectors.shape
    row_tiles = width // TILE
    n = n_blk * n_reader
    groups, slots = tile_rows.shape[1:]
    others = n_reader - 1
    dma = pltpu.SemaphoreType.DMA
    smem = pl.BlockSpec(memory_space=pltpu.SMEM)
    hbm = pl.BlockSpec(memory_space=pl.ANY)
    vmem = pl.BlockSpec(memory_space=pltpu.VMEM)
    body = functools.partial(kernel, n_blk, n_reader, n * width)
    return pl.pallas_call(
        body,
        out_shape=jax.ShapeDtypeStruct((vecs, width), jnp.float32),
        in_specs=[hbm, hbm, hbm, hbm, smem, smem],
        out_specs=vmem,
        scratch_shapes=[
            pltpu.VMEM((2, n, vecs, width), jnp.float32),
            pltpu.VMEM((n * row_tiles, 2 * vecs, TILE), jnp.bfloat16),
            pltpu.VMEM((groups, slots, TILE, TILE), jnp.float32),
            pltpu.VMEM((groups * slots, 2 * TILE, TILE), jnp.bfloat16),
            pltpu.VMEM((row_tiles, vecs, TILE), jnp.float32),
            pltpu.VMEM((vecs, width), jnp.float32),
            pltpu.VMEM((vecs, TILE), jnp.float32),
            pltpu.VMEM((PASSES, n - 1, 8, TILE), jnp.float32),
            pltpu.VMEM((PASSES, 8, TILE), jnp.float32),
            pltpu.SMEM((groups, slots), jnp.int32),
            pltpu.SMEM((groups, slots), jnp.int32),
            dma((groups,)), dma((3,)),
            dma((others, 2)), dma((2,)), dma((others,)), dma((others,)), dma,
            dma((others, 2)), dma((2,)), dma((others,)), dma((others,)),
            dma((2, others, 2)), dma((2, 2)), dma((2, others)), dma((2, others)), dma((2,)),
            dma((2, others, 2)), dma((2, 2)), dma((2, others)), dma((2, others)),
            dma((PASSES, n - 1)), dma((PASSES, n - 1)),
        ],
        compiler_params=pltpu.CompilerParams(
            collective_id=0, has_side_effects=True, vmem_limit_bytes=56 * 2**20
        ),
        cost_estimate=pl.CostEstimate(
            flops=PASSES * DEGREE * groups * slots * 8 * vecs * TILE * TILE,
            bytes_accessed=groups * slots * TILE * TILE * 4,
            transcendentals=0,
        ),
    )(vectors, ham_tiles, tile_rows, tile_cols, center, halfwidth)


def solution(mesh):
    n_blk, n_reader = mesh.shape["blk"], mesh.shape["reader"]
    return jax.shard_map(
        functools.partial(shards, n_blk, n_reader),
        mesh=mesh,
        in_specs=(
            P("bulk", ("blk", "reader")),
            P(("blk", "reader"), None, None, None, None),
            P(("blk", "reader"), None, None),
            P(("blk", "reader"), None, None),
            P(),
            P(),
        ),
        out_specs=P("bulk", ("blk", "reader")),
        check_vma=False,
    )
```
